32 devices in a mesh: slab: 2 (over y), blk: 4 (over z), bag: 2 (over x), sub: 2 (over core).
Axes of the slice: x: 2, y: 2, z: 4, core: 2. Of those that a mesh axis runs over, the one named last changes fastest.
Arguments:
- real_points: bfloat16 [64, 8192], P(None, ('slab', 'blk')), parts along dimension 1, may hold values from -4 to 4
- synth_points: bfloat16 [64, 8192], P(None, ('slab', 'blk')), parts along dimension 1, may hold values from -4 to 4
- real_cluster: int32 [8192], P(('slab', 'blk')), parts along dimension 0, may hold values from 0 to 3
- synth_cluster: int32 [8192], P(('slab', 'blk')), parts along dimension 0, may hold values from 0 to 3
- real_weight: int32 [32, 8192], P('bag', ('slab', 'blk')), parts along dimension 1, may hold values from 0 to 4
- synth_weight: int32 [32, 8192], P('bag', ('slab', 'blk')), parts along dimension 1, may hold values from 0 to 4
- pair_block: int32 [64, 2], P(('slab', 'blk', 'sub')), parts along dimension 0, may hold values from 0 to 7, as said below
- pair_row: int32 [64, 2], P(('slab', 'blk', 'sub')), parts along dimension 0, may hold values from 0 to 7
- pair_count: int32 [64], P(('slab', 'blk', 'sub')), parts along dimension 0, may hold values from 1 to 2, as said below
Outputs:
- real_potential: float32 [32, 8192], P('bag', ('slab', 'blk')), parts along dimension 1
- synth_potential: float32 [32, 8192], P('bag', ('slab', 'blk')), parts along dimension 1
The draws below stay inside these ranges and needn't reach their ends.
There are 2 independent parts, one for each index of `slab`. The reference program is written for one: setup_inputs(seed, part) draws one part's arguments, and reference() takes and returns one part's arrays. A program takes and returns all parts, laid end to end along the dimension named above; each array names one. Nothing has to cross between parts.
Inputs may be any that keep to these rules, and one draw needn't show every extreme that they name: `pair_block`: row 4 * (2 * b + s) + p belongs to the device at blk index b and sub index s; all listed pairs of the whole list are distinct. `pair_count`: in every draw all devices of one sub index list 2 pairs with one blk index.
All inputs are finite; a program needn't handle non-finite values.
Results may differ from the reference program's by a relative error of at most 0.0015.
Values may be sent and summed in bfloat16 or wider, within the bound.
A program may use at most 64 MiB of HBM per device.

```python
import math
import jax
import jax.numpy as jnp
from jax import lax

D = 64
BLOCK = 128
M = 32
XB = 8
PEER_CAP = 2
ITERS = 2
NPTS = 4096
N_BLK = 4
N_SUB = 2


def scaled_points(key, low_end, high_end):
    key_base, key_scale = jax.random.split(key, 2)
    base_draw = jax.random.truncated_normal(key_base, -4.0, 4.0, (D, NPTS), jnp.float32)
    point_scale = jnp.exp(jax.random.uniform(key_scale, (1, NPTS), jnp.float32, math.log(low_end), math.log(high_end)))
    values = base_draw * point_scale / math.sqrt(D)
    return jnp.clip(values, -4.0, 4.0).astype(jnp.bfloat16)


def draw_real_points(key, part):
    return scaled_points(jax.random.fold_in(key, 11), 0.6, 1.8)


def draw_synth_points(key, part):
    return scaled_points(jax.random.fold_in(key, 13), 0.6, 1.8)


def pair_lists(key):
    subkeys = jax.random.split(jax.random.fold_in(key, 29), 5)
    askers = N_BLK * N_SUB
    load_level = jax.random.randint(subkeys[0], (askers, 1), 1, PEER_CAP + 1)
    counts = 1 + jax.random.randint(subkeys[1], (askers, N_BLK), 0, 720720) % load_level
    hot_peer = jax.random.randint(subkeys[2], (), 0, N_BLK)
    hot_sub = jax.random.randint(subkeys[3], (), 0, N_SUB)
    asker_ids = jnp.arange(askers, dtype=jnp.int32)[:, None]
    peer_ids = jnp.arange(N_BLK, dtype=jnp.int32)[None, :]
    counts = jnp.where((asker_ids % N_SUB == hot_sub) & (peer_ids == hot_peer), PEER_CAP, counts)
    picked = jax.vmap(lambda one_key: jax.random.permutation(one_key, XB * XB)[:N_SUB * PEER_CAP])(jax.random.split(subkeys[4], N_BLK * N_BLK))
    picked = picked.reshape(N_BLK, N_BLK, PEER_CAP, N_SUB).transpose(0, 3, 1, 2).reshape(askers * N_BLK, PEER_CAP)
    return ((picked % XB).astype(jnp.int32), (picked // XB).astype(jnp.int32), counts.reshape(askers * N_BLK).astype(jnp.int32))


def draw_pair_block(key, part):
    return pair_lists(key)[0]


def draw_pair_row(key, part):
    return pair_lists(key)[1]


def draw_pair_count(key, part):
    return pair_lists(key)[2]


def place_ends(result, stream_key, smallest, high):
    dims = result.shape
    spot = [jax.random.randint(jax.random.fold_in(stream_key, axis), (), 0, dims[axis]) for axis in range(len(dims))]
    result = result.at[tuple(spot)].set(smallest)
    longest = dims.index(max(dims))
    spot[longest] = (spot[longest] + 1) % dims[longest]
    return result.at[tuple(spot)].set(high)


def setup_inputs(seed: int = 0, part: int = 0) -> dict:
    streams_of = jax.random.split(jax.random.key(seed), 10)
    own_keys = jax.random.split(jax.random.fold_in(streams_of[9], part), 10)
    real_points = draw_real_points(jax.random.fold_in(jax.random.fold_in(streams_of[9], part), 71), part)
    synth_points = draw_synth_points(jax.random.fold_in(jax.random.fold_in(streams_of[9], part), 71), part)
    real_cluster = place_ends(jax.random.randint(own_keys[2], (NPTS,), 0, 4), jax.random.fold_in(own_keys[2], 1), 0, 3).astype(jnp.int32)
    synth_cluster = place_ends(jax.random.randint(own_keys[3], (NPTS,), 0, 4), jax.random.fold_in(own_keys[3], 1), 0, 3).astype(jnp.int32)
    real_weight = place_ends(jax.random.randint(own_keys[4], (M, NPTS), 0, 5), jax.random.fold_in(own_keys[4], 1), 0, 4).astype(jnp.int32)
    synth_weight = place_ends(jax.random.randint(own_keys[5], (M, NPTS), 0, 5), jax.random.fold_in(own_keys[5], 1), 0, 4).astype(jnp.int32)
    pair_block = draw_pair_block(jax.random.fold_in(jax.random.fold_in(streams_of[9], part), 71), part)
    pair_row = draw_pair_row(jax.random.fold_in(jax.random.fold_in(streams_of[9], part), 71), part)
    pair_count = draw_pair_count(jax.random.fold_in(jax.random.fold_in(streams_of[9], part), 71), part)
    return dict(real_points=real_points, synth_points=synth_points, real_cluster=real_cluster, synth_cluster=synth_cluster, real_weight=real_weight, synth_weight=synth_weight, pair_block=pair_block, pair_row=pair_row, pair_count=pair_count)


SMOOTH = 0.1
PENALTY = 0.3
SENTINEL = -1.0e30


def finish(log_weight, block_top, summed):
    spread = jnp.where(summed > 0.5, block_top + jnp.log(jnp.maximum(summed, 0.5)), 0.0)
    return SMOOTH * log_weight - SMOOTH * spread


def reference(real_points, synth_points, real_cluster, synth_cluster, real_weight, synth_weight, pair_block, pair_row, pair_count):
    total_blocks = XB * N_BLK
    listings = N_BLK * N_SUB * N_BLK
    listing = jnp.arange(listings, dtype=jnp.int32)
    asking = listing // N_BLK // N_SUB
    owners = listing % N_BLK
    usable = (jnp.arange(PEER_CAP, dtype=jnp.int32)[None, :] < pair_count[:, None]).reshape(-1)
    row_ids = (asking[:, None] * XB + pair_row).reshape(-1).astype(jnp.int32)
    col_ids = (owners[:, None] * XB + pair_block).reshape(-1).astype(jnp.int32)
    row_seg = jnp.where(usable, row_ids, total_blocks).astype(jnp.int32)
    col_seg = jnp.where(usable, col_ids, total_blocks).astype(jnp.int32)
    real_three = real_points.reshape(D, total_blocks, BLOCK)
    synth_three = synth_points.reshape(D, total_blocks, BLOCK)
    real_tags = real_cluster.reshape(total_blocks, BLOCK)
    synth_tags = synth_cluster.reshape(total_blocks, BLOCK)
    log_real = jnp.log(real_weight.astype(jnp.float32) + 0.5).reshape(M, total_blocks, BLOCK)
    log_synth = jnp.log(synth_weight.astype(jnp.float32) + 0.5).reshape(M, total_blocks, BLOCK)

    def block_cost(row_id, col_id):
        real_block = lax.dynamic_index_in_dim(real_three, row_id, 1, keepdims=False)
        synth_block = lax.dynamic_index_in_dim(synth_three, col_id, 1, keepdims=False)
        inner_prod = jnp.dot(real_block.T, synth_block, preferred_element_type=jnp.float32)
        real_sq = jnp.sum(jnp.square(real_block.astype(jnp.float32)), axis=0)
        synth_sq = jnp.sum(jnp.square(synth_block.astype(jnp.float32)), axis=0)
        real_tag = lax.dynamic_index_in_dim(real_tags, row_id, 0, keepdims=False)
        synth_tag = lax.dynamic_index_in_dim(synth_tags, col_id, 0, keepdims=False)
        differ = (real_tag[:, None] != synth_tag[None, :]).astype(jnp.float32)
        return 0.5 * real_sq[:, None] + 0.5 * synth_sq[None, :] - inner_prod + PENALTY * differ

    def fold_all(highest, mass_sum, segment):
        block_top = jnp.full((total_blocks + 1, M, BLOCK), SENTINEL, jnp.float32).at[segment].max(highest)
        scaled = mass_sum * jnp.exp(highest - block_top[segment])
        summed = jnp.zeros((total_blocks + 1, M, BLOCK), jnp.float32).at[segment].add(scaled)
        return jnp.transpose(block_top[:total_blocks], (1, 0, 2)), jnp.transpose(summed[:total_blocks], (1, 0, 2))

    synth_pot = jnp.zeros((M, total_blocks, BLOCK), jnp.float32)
    real_pot = jnp.zeros((M, total_blocks, BLOCK), jnp.float32)
    for sweep_index in range(ITERS):
        def row_part(pair_ids, synth_now=synth_pot):
            pair_cost = block_cost(pair_ids[0], pair_ids[1])
            panel_rows = lax.dynamic_index_in_dim(synth_now, pair_ids[1], 1, keepdims=False)
            scores = (panel_rows[:, None, :] - pair_cost[None]) / SMOOTH
            highest = jnp.max(scores, axis=2)
            return highest, jnp.sum(jnp.exp(scores - highest[:, :, None]), axis=2)

        highest, mass_sum = lax.map(row_part, (row_ids, col_ids))
        block_top, summed = fold_all(highest, mass_sum, row_seg)
        real_pot = finish(log_real, block_top, summed)

        def col_part(pair_ids, real_now=real_pot):
            pair_cost = block_cost(pair_ids[0], pair_ids[1])
            panel_rows = lax.dynamic_index_in_dim(real_now, pair_ids[0], 1, keepdims=False)
            scores = (panel_rows[:, :, None] - pair_cost[None]) / SMOOTH
            highest = jnp.max(scores, axis=1)
            return highest, jnp.sum(jnp.exp(scores - highest[:, None, :]), axis=1)

        highest, mass_sum = lax.map(col_part, (row_ids, col_ids))
        block_top, summed = fold_all(highest, mass_sum, col_seg)
        synth_pot = finish(log_synth, block_top, summed)
    return real_pot.reshape(M, total_blocks * BLOCK), synth_pot.reshape(M, total_blocks * BLOCK)
```

```python
import functools
import math

import jax
import jax.numpy as jnp
import ml_dtypes
from jax import lax
from jax.experimental import pallas as pl
from jax.experimental.pallas import tpu as pltpu
from jax.sharding import PartitionSpec as P

BLOCK = 128
SMOOTH = 0.1
PENALTY = 0.3
SENTINEL = -1e30
ALPHA = 1.0 / (SMOOTH * math.log(2.0))
HIGH = float(ml_dtypes.bfloat16(PENALTY))
LOW = float(ml_dtypes.bfloat16(PENALTY - HIGH))
TILE = 16
MESH = pl.DeviceIdType.MESH
F32 = jnp.float32
BF16 = jnp.bfloat16


def split3(value):
    first = value.astype(BF16).astype(F32)
    second = (value - first).astype(BF16).astype(F32)
    third = (value - first - second).astype(BF16).astype(F32)
    return first, second, third


def put_rows(tile, value, start):
    row = lax.broadcasted_iota(jnp.int32, tile.shape, 0)
    for offset, part in enumerate(split3(value)):
        tile = jnp.where(row == start + offset, part, tile)
    return tile


def fold_max(tops, masks):
    best = jnp.full((masks[0].shape[0], BLOCK), SENTINEL, F32)
    for top, mask in zip(tops, masks):
        best = jnp.maximum(best, jnp.where(mask, top, SENTINEL))
    return best


def kernel(
    peers, cap, blocks, marginals, feats,
    x_ref, y_ref, xc_ref, yc_ref, xw_ref, yw_ref, pb_ref, pr_ref, pc_ref,
    real_out, synth_out,
    xf, xt, xu, wr, ys, req_out, req_in, y_out, y_in,
    s1_out, s1_in, c_out, c_in, own_a, own_t, rep_out, rep_in, s2_out, s2_in, bw,
    big_send, big_recv, send, recv, s_send, s_recv,
):
    slab, blk, bag, sub = (lax.axis_index(name) for name in ("slab", "blk", "bag", "sub"))
    other = 1 - sub
    mine = sub * peers + blk
    group = 2 * peers

    def device(p, s):
        return (slab, p, bag, s)

    others = [(lax.rem(blk + d, peers), s) for d in range(1, peers) for s in (sub, other)]
    others.append((blk, other))

    barrier = pltpu.get_barrier_semaphore()
    for p, s in others:
        pl.semaphore_signal(barrier, inc=1, device_id=device(p, s), device_id_type=MESH)

    for p in range(peers):
        for c in range(cap):
            listed = c < pc_ref[p]
            wanted = jnp.where(listed, pb_ref[p, c], 99).astype(F32)
            req_out[p, c] = jnp.full((TILE, BLOCK), wanted, F32).astype(BF16)
    req_in[mine] = req_out[blk]
    pl.semaphore_wait(barrier, len(others))

    pending = []

    def post(src, dst, send_sem, recv_sem, target):
        copy = pltpu.make_async_remote_copy(
            src_ref=src, dst_ref=dst, send_sem=send_sem, recv_sem=recv_sem,
            device_id=target, device_id_type=MESH,
        )
        copy.start()
        pending.append(copy)

    def arrived(dst, send_sem, recv_sem):
        pltpu.make_async_remote_copy(
            src_ref=dst, dst_ref=dst, send_sem=send_sem, recv_sem=recv_sem,
            device_id=device(blk, other), device_id_type=MESH,
        ).wait_recv()

    for p, s in others:
        post(req_out.at[p], req_in.at[mine], big_send.at[0, s * peers + p], big_recv.at[0, mine],
             device(p, s))

    row = lax.broadcasted_iota(jnp.int32, (TILE, BLOCK), 0)
    cluster = jnp.where(row < 10, row - 6, row - 10)
    for n in range(blocks):
        lanes = slice(n * BLOCK, (n + 1) * BLOCK)
        y = y_ref[:, lanes]
        y32 = y.astype(F32)
        fy = -0.5 * jnp.sum(y32 * y32, axis=0, keepdims=True)
        hit = (row >= 6) & (row < 14) & (cluster == yc_ref[n : n + 1, :])
        tile = jnp.where(hit, jnp.where(row < 10, HIGH, LOW), 0.0)
        tile = jnp.where(row < 3, 1.0, tile)
        tile = put_rows(tile, fy, 3)
        ys[n, 0:feats] = y
        ys[n, feats:] = tile.astype(BF16)
    for n in range(blocks):
        lanes = slice(n * BLOCK, (n + 1) * BLOCK)
        x = x_ref[:, lanes]
        x32 = x.astype(F32)
        fx = -0.5 * jnp.sum(x32 * x32, axis=0, keepdims=True) - PENALTY
        hit = (row >= 6) & (row < 14) & (cluster == xc_ref[n : n + 1, :])
        tile = jnp.where(hit, 1.0, 0.0)
        tile = jnp.where((row >= 3) & (row < 6), 1.0, tile)
        tile = put_rows(tile, fx, 0)
        xf[n] = x
        xt[n] = tile.astype(BF16)
        wr[n] = (xw_ref[:, lanes].astype(F32) + 0.5).astype(BF16)

    def answer(p):
        src = sub * peers + p
        for c in range(cap):
            asked = req_in[src, c]
            value = ys[0].reshape(-1, TILE, BLOCK)
            for n in range(1, blocks):
                value = jnp.where((asked == n)[None], ys[n].reshape(-1, TILE, BLOCK), value)
            yield c, value.reshape(-1, BLOCK)

    for d in range(1, peers):
        p = lax.rem(blk + d, peers)
        src = sub * peers + p
        arrived(req_in.at[src], big_send.at[0, src], big_recv.at[0, src])
        for c, value in answer(p):
            y_out[p, c] = value
        post(y_out.at[p], y_in.at[blk], send.at[0, p], recv.at[0, blk], device(p, sub))
    for c, value in answer(blk):
        y_in[blk, c] = value

    order = [lax.rem(blk + d, peers) for d in range(peers)]
    far_first = order[1:] + order[:1]
    eight = lax.broadcasted_iota(jnp.int32, (blocks, BLOCK), 0)

    def row_of(p, c):
        return pr_ref[p, c]

    def row_mask(p, c):
        return eight == jnp.where(c < pc_ref[p], pr_ref[p, c], blocks)

    contract = (((0,), (0,)), ((), ()))
    slots = [(p, c) for p in order for c in range(cap)]
    masks = [row_mask(p, c) for p, c in slots]

    tops, sums = [], []
    for d, p in enumerate(order):
        if d:
            arrived(y_in.at[p], send.at[0, p], recv.at[0, p])
        for c in range(cap):
            r = row_of(p, c)
            x = jnp.concatenate([xf[r], xt[r]], axis=0)
            z = lax.dot_general(y_in[p, c], x, contract, preferred_element_type=F32)
            top = jnp.max(z, axis=0, keepdims=True)
            tops.append(top)
            sums.append(jnp.sum(jnp.exp2(ALPHA * (z - top)), axis=0, keepdims=True))
    best = fold_max(tops, masks)
    total = jnp.zeros((blocks, BLOCK), F32)
    for top, part, mask in zip(tops, sums, masks):
        total += jnp.where(mask, jnp.exp2(ALPHA * (top - best)) * part, 0.0)
    s1_out[0] = best
    s1_out[1] = total
    post(s1_out, s1_in, s_send.at[0], s_recv.at[0], device(blk, other))
    arrived(s1_in, s_send.at[0], s_recv.at[0])
    peak = jnp.maximum(best, s1_in[0])
    total = total * jnp.exp2(ALPHA * (best - peak)) + s1_in[1] * jnp.exp2(ALPHA * (s1_in[0] - peak))
    used = peak > 0.5 * SENTINEL
    level = jnp.where(used, peak + jnp.log(jnp.where(used, total, 1.0)) * SMOOTH, 0.0)

    def shift_rows(level):
        for n in range(blocks):
            lanes = slice(n * BLOCK, (n + 1) * BLOCK)
            tile = xt[n].astype(F32)
            base = tile[0:1] + tile[1:2] + tile[2:3]
            xu[n] = put_rows(tile, base - level[n : n + 1], 0).astype(BF16)

    def col_sweep(turn, factor):
        for d, p in enumerate(far_first):
            for c in range(cap):
                r = row_of(p, c)
                x = jnp.concatenate([xf[r], xu[r]], axis=0)
                z = lax.dot_general(x, y_in[p, c], contract, preferred_element_type=F32)
                top = jnp.max(z, axis=0, keepdims=True)
                table = jnp.exp2(ALPHA * (z - top)).astype(BF16)
                mass = jnp.dot(factor[r], table, preferred_element_type=F32)
                wide = jnp.broadcast_to(top, (8, BLOCK))
                c_out[turn, p, c, 0:marginals] = mass
                c_out[turn, p, c, marginals:] = wide
                if d == peers - 1:
                    c_in[turn, mine, c, 0:marginals] = mass
                    c_in[turn, mine, c, marginals:] = wide
            for s in (sub, other):
                if d == peers - 1 and s is sub:
                    continue
                post(c_out.at[turn, p], c_in.at[turn, mine], big_send.at[1 + turn, s * peers + p],
                     big_recv.at[1 + turn, mine], device(p, s))

    def col_fold(turn):
        sources = [mine, other * peers + blk]
        sources += [s * peers + p for p in order[1:] for s in (sub, other)]
        tops, hits = [], []
        for d, src in enumerate(sources):
            if d:
                arrived(c_in.at[turn, src], big_send.at[1 + turn, src], big_recv.at[1 + turn, src])
                if turn == 0 and d % 2 == 1:
                    arrived(req_in.at[src], big_send.at[0, src], big_recv.at[0, src])
            for c in range(cap):
                tops.append(c_in[turn, src, c, marginals:][0:1])
                asked = req_in[src, c].astype(F32)[0:1]
                hits.append(asked == eight.astype(F32))
        best = fold_max(tops, hits)
        totals = [jnp.zeros((marginals, BLOCK), F32) for _ in range(blocks)]
        k = 0
        for src in sources:
            for c in range(cap):
                scale = jnp.where(hits[k], jnp.exp2(ALPHA * (tops[k] - best)), 0.0)
                mass = c_in[turn, src, c, 0:marginals]
                for n in range(blocks):
                    totals[n] += scale[n : n + 1] * mass
                k += 1
        return best, totals

    shift_rows(level)
    col_sweep(0, wr)
    best, totals = col_fold(0)
    used = best > 0.5 * SENTINEL
    level = jnp.where(used, best, 0.0)
    for n in range(blocks):
        lanes = slice(n * BLOCK, (n + 1) * BLOCK)
        some = used[n : n + 1]
        weight = yw_ref[:, lanes].astype(F32) + 0.5
        own_a[n] = (weight / jnp.where(some, totals[n], 1.0)).astype(BF16)
        tile = ys[n, feats:].astype(F32)
        base = tile[3:4] + tile[4:5] + tile[5:6]
        own_t[n] = put_rows(tile, base - level[n : n + 1], 3).astype(BF16)
    for d, p in enumerate(far_first):
        src = sub * peers + p
        for c in range(cap):
            asked = req_in[src, c]
            factor, tile = own_a[0], own_t[0]
            for n in range(1, blocks):
                hit = asked == n
                factor = jnp.where(hit, own_a[n], factor)
                tile = jnp.where(hit, own_t[n], tile)
            target = rep_in if d == peers - 1 else rep_out
            target[p, c, 0] = factor
            target[p, c, 1] = tile
        if d < peers - 1:
            post(rep_out.at[p], rep_in.at[blk], send.at[1, p], recv.at[1, blk], device(p, sub))

    tops, masses = [], []
    for d, p in enumerate(order):
        if d:
            arrived(rep_in.at[p], send.at[1, p], recv.at[1, p])
        for c in range(cap):
            r = row_of(p, c)
            x = jnp.concatenate([xf[r], xt[r]], axis=0)
            y = jnp.concatenate([y_in[p, c][0:feats], rep_in[p, c, 1]], axis=0)
            z = lax.dot_general(y, x, contract, preferred_element_type=F32)
            top = jnp.max(z, axis=0, keepdims=True)
            table = jnp.exp2(ALPHA * (z - top)).astype(BF16)
            tops.append(top)
            masses.append(jnp.dot(rep_in[p, c, 0], table, preferred_element_type=F32))
    best = fold_max(tops, masks)
    totals = [jnp.zeros((marginals, BLOCK), F32) for _ in range(blocks)]
    for top, mass, mask in zip(tops, masses, masks):
        scale = jnp.where(mask, jnp.exp2(ALPHA * (top - best)), 0.0)
        for n in range(blocks):
            totals[n] += scale[n : n + 1] * mass
    per = marginals // 8
    for n in range(blocks):
        s2_out[1 + per * n : 1 + per * (n + 1)] = totals[n].reshape(per, 8, BLOCK)
    s2_out[0] = best
    post(s2_out, s2_in, s_send.at[1], s_recv.at[1], device(blk, other))
    arrived(s2_in, s_send.at[1], s_recv.at[1])
    theirs = s2_in[0]
    peak = jnp.maximum(best, theirs)
    scale_own, scale_far = jnp.exp2(ALPHA * (best - peak)), jnp.exp2(ALPHA * (theirs - peak))
    used = peak > 0.5 * SENTINEL
    level = jnp.where(used, peak, 0.0)
    sums = []
    for n in range(blocks):
        lanes = slice(n * BLOCK, (n + 1) * BLOCK)
        far = s2_in[1 + per * n : 1 + per * (n + 1)].reshape(marginals, BLOCK)
        total = totals[n] * scale_own[n : n + 1] + far * scale_far[n : n + 1]
        total = jnp.where(used[n : n + 1], total, 1.0)
        weight = xw_ref[:, lanes].astype(F32) + 0.5
        bw[n] = (weight / total).astype(BF16)
        sums.append(total)
    shift_rows(level)
    col_sweep(1, bw)
    for n in range(blocks):
        lanes = slice(n * BLOCK, (n + 1) * BLOCK)
        weight = xw_ref[:, lanes].astype(F32) + 0.5
        real_out[:, lanes] = SMOOTH * (jnp.log(weight) - jnp.log(sums[n])) - level[n : n + 1]
    best, totals = col_fold(1)
    used = best > 0.5 * SENTINEL
    level = jnp.where(used, best, 0.0)
    for n in range(blocks):
        lanes = slice(n * BLOCK, (n + 1) * BLOCK)
        weight = yw_ref[:, lanes].astype(F32) + 0.5
        total = jnp.where(used[n : n + 1], totals[n], 1.0)
        synth_out[:, lanes] = SMOOTH * (jnp.log(weight) - jnp.log(total)) - level[n : n + 1]
    for copy in pending:
        copy.wait_send()


def shards(
    real_points, synth_points, real_cluster, synth_cluster, real_weight, synth_weight,
    pair_block, pair_row, pair_count,
):
    feats, count = real_points.shape
    blocks = count // BLOCK
    kept = real_weight.shape[0]
    marginals = -(-kept // TILE) * TILE
    if marginals > kept:
        grow = ((0, marginals - kept), (0, 0))
        real_weight, synth_weight = jnp.pad(real_weight, grow), jnp.pad(synth_weight, grow)
    peers, cap = pair_block.shape
    group = 2 * peers
    depth = feats + TILE
    vmem = pl.BlockSpec(memory_space=pltpu.VMEM)
    smem = pl.BlockSpec(memory_space=pltpu.SMEM)
    real_pot, synth_pot = pl.pallas_call(
        functools.partial(kernel, peers, cap, blocks, marginals, feats),
        out_shape=(
            jax.ShapeDtypeStruct((marginals, count), F32),
            jax.ShapeDtypeStruct((marginals, count), F32),
        ),
        in_specs=[vmem] * 6 + [smem] * 3,
        out_specs=(vmem, vmem),
        scratch_shapes=[
            pltpu.VMEM((blocks, feats, BLOCK), BF16),
            pltpu.VMEM((blocks, TILE, BLOCK), BF16),
            pltpu.VMEM((blocks, TILE, BLOCK), BF16),
            pltpu.VMEM((blocks, marginals, BLOCK), BF16),
            pltpu.VMEM((blocks, depth, BLOCK), BF16),
            pltpu.VMEM((peers, cap, TILE, BLOCK), BF16),
            pltpu.VMEM((group, cap, TILE, BLOCK), BF16),
            pltpu.VMEM((peers, cap, depth, BLOCK), BF16),
            pltpu.VMEM((peers, cap, depth, BLOCK), BF16),
            pltpu.VMEM((2, blocks, BLOCK), F32),
            pltpu.VMEM((2, blocks, BLOCK), F32),
            pltpu.VMEM((2, peers, cap, marginals + 8, BLOCK), F32),
            pltpu.VMEM((2, group, cap, marginals + 8, BLOCK), F32),
            pltpu.VMEM((blocks, marginals, BLOCK), BF16),
            pltpu.VMEM((blocks, TILE, BLOCK), BF16),
            pltpu.VMEM((peers, cap, 2, TILE, BLOCK), BF16),
            pltpu.VMEM((peers, cap, 2, TILE, BLOCK), BF16),
            pltpu.VMEM((1 + marginals // 8 * blocks, 8, BLOCK), F32),
            pltpu.VMEM((1 + marginals // 8 * blocks, 8, BLOCK), F32),
            pltpu.VMEM((blocks, marginals, BLOCK), BF16),
            pltpu.SemaphoreType.DMA((3, group)),
            pltpu.SemaphoreType.DMA((3, group)),
            pltpu.SemaphoreType.DMA((2, peers)),
            pltpu.SemaphoreType.DMA((2, peers)),
            pltpu.SemaphoreType.DMA((2,)),
            pltpu.SemaphoreType.DMA((2,)),
        ],
        compiler_params=pltpu.CompilerParams(
            collective_id=0, has_side_effects=True, vmem_limit_bytes=32 * 1024 * 1024
        ),
    )(
        real_points, synth_points,
        real_cluster.reshape(blocks, BLOCK), synth_cluster.reshape(blocks, BLOCK),
        real_weight, synth_weight, pair_block, pair_row, pair_count,
    )
    return real_pot[:kept], synth_pot[:kept]


def solution(mesh):
    placed = (
        P(None, ("slab", "blk")),
        P(None, ("slab", "blk")),
        P(("slab", "blk")),
        P(("slab", "blk")),
        P("bag", ("slab", "blk")),
        P("bag", ("slab", "blk")),
        P(("slab", "blk", "sub"), None),
        P(("slab", "blk", "sub"), None),
        P(("slab", "blk", "sub")),
    )
    return jax.shard_map(
        shards,
        mesh=mesh,
        in_specs=placed,
        out_specs=(P("bag", ("slab", "blk")), P("bag", ("slab", "blk"))),
        check_vma=False,
    )
```

```python
import functools
import math

import jax
import jax.numpy as jnp
import ml_dtypes
from jax import lax
from jax.experimental import pallas as pl
from jax.experimental.pallas import tpu as pltpu
from jax.sharding import PartitionSpec as P

BLOCK = 128
SMOOTH = 0.1
PENALTY = 0.3
SENTINEL = -1e30
ALPHA = 1.0 / (SMOOTH * math.log(2.0))
HIGH = float(ml_dtypes.bfloat16(PENALTY))
LOW = float(ml_dtypes.bfloat16(PENALTY - HIGH))
TILE = 16
MESH = pl.DeviceIdType.MESH
F32 = jnp.float32
BF16 = jnp.bfloat16


def split3(value):
    first = value.astype(BF16).astype(F32)
    second = (value - first).astype(BF16).astype(F32)
    third = (value - first - second).astype(BF16).astype(F32)
    return first, second, third


def put_rows(tile, value, start):
    row = lax.broadcasted_iota(jnp.int32, tile.shape, 0)
    for offset, part in enumerate(split3(value)):
        tile = jnp.where(row == start + offset, part, tile)
    return tile


def fold_max(tops, masks):
    best = jnp.full((masks[0].shape[0], BLOCK), SENTINEL, F32)
    for top, mask in zip(tops, masks):
        best = jnp.maximum(best, jnp.where(mask, top, SENTINEL))
    return best


def kernel(
    peers, cap, blocks, marginals, feats,
    x_hbm, y_hbm, xc_hbm, yc_hbm, xw_hbm, yw_hbm, pb_hbm, pr_hbm, pc_hbm,
    real_out, synth_out,
    x_ref, y_ref, xc_ref, yc_ref, xw_ref, yw_ref, pb_ref, pr_ref, pc_ref, in_sem,
    xf, xt, xu, wr, ys, req_out, req_in, y_out, y_in,
    s1_out, s1_in, c_out, c_in, own_a, own_t, rep_out, rep_in, s2_out, s2_in, bw,
    big_send, big_recv, send, recv, s_send, s_recv,
):
    slab, blk, bag, sub = (lax.axis_index(name) for name in ("slab", "blk", "bag", "sub"))
    loads = [
        pltpu.make_async_copy(src, dst, in_sem.at[k])
        for k, (src, dst) in enumerate((
            (pb_hbm, pb_ref), (pc_hbm, pc_ref), (pr_hbm, pr_ref), (y_hbm, y_ref), (yc_hbm, yc_ref),
            (x_hbm, x_ref), (xc_hbm, xc_ref), (xw_hbm, xw_ref), (yw_hbm, yw_ref),
        ))
    ]
    for load in loads:
        load.start()
    other = 1 - sub
    mine = sub * peers + blk
    group = 2 * peers

    def device(p, s):
        return (slab, p, bag, s)

    others = [(lax.rem(blk + d, peers), s) for d in range(1, peers) for s in (sub, other)]
    others.append((blk, other))

    barrier = pltpu.get_barrier_semaphore()
    for p, s in others:
        pl.semaphore_signal(barrier, inc=1, device_id=device(p, s), device_id_type=MESH)

    for load in loads[:3]:
        load.wait()
    for p in range(peers):
        for c in range(cap):
            listed = c < pc_ref[p]
            wanted = jnp.where(listed, pb_ref[c, p], 99).astype(F32)
            req_out[p, c] = jnp.full((TILE, BLOCK), wanted, F32).astype(BF16)
    req_in[mine] = req_out[blk]
    pl.semaphore_wait(barrier, len(others))

    pending = []

    def post(src, dst, send_sem, recv_sem, target):
        copy = pltpu.make_async_remote_copy(
            src_ref=src, dst_ref=dst, send_sem=send_sem, recv_sem=recv_sem,
            device_id=target, device_id_type=MESH,
        )
        copy.start()
        pending.append(copy)

    def arrived(dst, send_sem, recv_sem):
        pltpu.make_async_remote_copy(
            src_ref=dst, dst_ref=dst, send_sem=send_sem, recv_sem=recv_sem,
            device_id=device(blk, other), device_id_type=MESH,
        ).wait_recv()

    for p, s in others:
        post(req_out.at[p], req_in.at[mine], big_send.at[0, s * peers + p], big_recv.at[0, mine],
             device(p, s))

    for load in loads[3:]:
        load.wait()
    row = lax.broadcasted_iota(jnp.int32, (TILE, BLOCK), 0)
    cluster = jnp.where(row < 10, row - 6, row - 10)
    for n in range(blocks):
        lanes = slice(n * BLOCK, (n + 1) * BLOCK)
        y = y_ref[:, lanes]
        y32 = y.astype(F32)
        fy = -0.5 * jnp.sum(y32 * y32, axis=0, keepdims=True)
        hit = (row >= 6) & (row < 14) & (cluster == yc_ref[n : n + 1, :])
        tile = jnp.where(hit, jnp.where(row < 10, HIGH, LOW), 0.0)
        tile = jnp.where(row < 3, 1.0, tile)
        tile = put_rows(tile, fy, 3)
        ys[n, 0:feats] = y
        ys[n, feats:] = tile.astype(BF16)
    for n in range(blocks):
        lanes = slice(n * BLOCK, (n + 1) * BLOCK)
        x = x_ref[:, lanes]
        x32 = x.astype(F32)
        fx = -0.5 * jnp.sum(x32 * x32, axis=0, keepdims=True) - PENALTY
        hit = (row >= 6) & (row < 14) & (cluster == xc_ref[n : n + 1, :])
        tile = jnp.where(hit, 1.0, 0.0)
        tile = jnp.where((row >= 3) & (row < 6), 1.0, tile)
        tile = put_rows(tile, fx, 0)
        xf[n] = x
        xt[n] = tile.astype(BF16)
        wr[n] = (xw_ref[:, lanes].astype(F32) + 0.5).astype(BF16)

    def answer(p):
        src = sub * peers + p
        for c in range(cap):
            asked = req_in[src, c]
            value = ys[0].reshape(-1, TILE, BLOCK)
            for n in range(1, blocks):
                value = jnp.where((asked == n)[None], ys[n].reshape(-1, TILE, BLOCK), value)
            yield c, value.reshape(-1, BLOCK)

    for d in range(1, peers):
        p = lax.rem(blk + d, peers)
        src = sub * peers + p
        arrived(req_in.at[src], big_send.at[0, src], big_recv.at[0, src])
        for c, value in answer(p):
            y_out[p, c] = value
        post(y_out.at[p], y_in.at[blk], send.at[0, p], recv.at[0, blk], device(p, sub))
    for c, value in answer(blk):
        y_in[blk, c] = value

    order = [lax.rem(blk + d, peers) for d in range(peers)]
    far_first = order[1:] + order[:1]
    eight = lax.broadcasted_iota(jnp.int32, (blocks, BLOCK), 0)

    def row_of(p, c):
        return pr_ref[c, p]

    def row_mask(p, c):
        return eight == jnp.where(c < pc_ref[p], pr_ref[c, p], blocks)

    contract = (((0,), (0,)), ((), ()))
    slots = [(p, c) for p in order for c in range(cap)]
    masks = [row_mask(p, c) for p, c in slots]

    tops, sums = [], []
    for d, p in enumerate(order):
        if d == 1:
            for q in order[1:]:
                arrived(y_in.at[q], send.at[0, q], recv.at[0, q])
        for c in range(cap):
            r = row_of(p, c)
            x = jnp.concatenate([xf[r], xt[r]], axis=0)
            z = lax.dot_general(y_in[p, c], x, contract, preferred_element_type=F32)
            top = jnp.max(z, axis=0, keepdims=True)
            tops.append(top)
            sums.append(jnp.sum(jnp.exp2(ALPHA * (z - top)), axis=0, keepdims=True))
    best = fold_max(tops, masks)
    total = jnp.zeros((blocks, BLOCK), F32)
    for top, part, mask in zip(tops, sums, masks):
        total += jnp.where(mask, jnp.exp2(ALPHA * (top - best)) * part, 0.0)
    s1_out[0] = best
    s1_out[1] = total
    post(s1_out, s1_in, s_send.at[0], s_recv.at[0], device(blk, other))
    arrived(s1_in, s_send.at[0], s_recv.at[0])
    peak = jnp.maximum(best, s1_in[0])
    total = total * jnp.exp2(ALPHA * (best - peak)) + s1_in[1] * jnp.exp2(ALPHA * (s1_in[0] - peak))
    used = peak > 0.5 * SENTINEL
    level = jnp.where(used, peak + jnp.log(jnp.where(used, total, 1.0)) * SMOOTH, 0.0)

    def shift_rows(level):
        for n in range(blocks):
            lanes = slice(n * BLOCK, (n + 1) * BLOCK)
            tile = xt[n].astype(F32)
            base = tile[0:1] + tile[1:2] + tile[2:3]
            xu[n] = put_rows(tile, base - level[n : n + 1], 0).astype(BF16)

    def col_sweep(turn, factor):
        def masses(p):
            for c in range(cap):
                r = row_of(p, c)
                x = jnp.concatenate([xf[r], xu[r]], axis=0)
                z = lax.dot_general(x, y_in[p, c], contract, preferred_element_type=F32)
                top = jnp.max(z, axis=0, keepdims=True)
                table = jnp.exp2(ALPHA * (z - top)).astype(BF16)
                mass = jnp.dot(factor[r], table, preferred_element_type=F32)
                yield c, mass, jnp.broadcast_to(top, (8, BLOCK))

        def deliver(p, s):
            post(c_out.at[turn, p], c_in.at[turn, mine], big_send.at[1 + turn, s * peers + p],
                 big_recv.at[1 + turn, mine], device(p, s))

        for p in order[1:]:
            for c, mass, top in masses(p):
                c_out[turn, p, c, 0:marginals] = mass
                c_out[turn, p, c, marginals:] = top
        for p in order[1:]:
            deliver(p, sub)
            deliver(p, other)
        for c, mass, top in masses(blk):
            for target in (c_out.at[turn, blk, c], c_in.at[turn, mine, c]):
                target[0:marginals] = mass
                target[marginals:] = top
        deliver(blk, other)

    def col_fold(turn):
        sources = [mine, other * peers + blk]
        sources += [s * peers + p for p in order[1:] for s in (sub, other)]
        tops, hits = [], []
        for d, src in enumerate(sources):
            if d:
                arrived(c_in.at[turn, src], big_send.at[1 + turn, src], big_recv.at[1 + turn, src])
                if turn == 0 and d % 2 == 1:
                    arrived(req_in.at[src], big_send.at[0, src], big_recv.at[0, src])
            for c in range(cap):
                tops.append(c_in[turn, src, c, marginals:][0:1])
                asked = req_in[src, c].astype(F32)[0:1]
                hits.append(asked == eight.astype(F32))
        best = fold_max(tops, hits)
        totals = [jnp.zeros((marginals, BLOCK), F32) for _ in range(blocks)]
        k = 0
        for src in sources:
            for c in range(cap):
                scale = jnp.where(hits[k], jnp.exp2(ALPHA * (tops[k] - best)), 0.0)
                mass = c_in[turn, src, c, 0:marginals]
                for n in range(blocks):
                    totals[n] += scale[n : n + 1] * mass
                k += 1
        return best, totals

    shift_rows(level)
    col_sweep(0, wr)
    best, totals = col_fold(0)
    used = best > 0.5 * SENTINEL
    level = jnp.where(used, best, 0.0)
    for n in range(blocks):
        lanes = slice(n * BLOCK, (n + 1) * BLOCK)
        some = used[n : n + 1]
        weight = yw_ref[:, lanes].astype(F32) + 0.5
        own_a[n] = (weight / jnp.where(some, totals[n], 1.0)).astype(BF16)
        tile = ys[n, feats:].astype(F32)
        base = tile[3:4] + tile[4:5] + tile[5:6]
        own_t[n] = put_rows(tile, base - level[n : n + 1], 3).astype(BF16)
    for d, p in enumerate(far_first):
        src = sub * peers + p
        for c in range(cap):
            asked = req_in[src, c]
            factor, tile = own_a[0], own_t[0]
            for n in range(1, blocks):
                hit = asked == n
                factor = jnp.where(hit, own_a[n], factor)
                tile = jnp.where(hit, own_t[n], tile)
            target = rep_in if d == peers - 1 else rep_out
            target[p, c, 0] = factor
            target[p, c, 1] = tile
        if d < peers - 1:
            post(rep_out.at[p], rep_in.at[blk], send.at[1, p], recv.at[1, blk], device(p, sub))

    tops, masses = [], []
    for d, p in enumerate(order):
        if d == 1:
            for q in order[1:]:
                arrived(rep_in.at[q], send.at[1, q], recv.at[1, q])
        for c in range(cap):
            r = row_of(p, c)
            x = jnp.concatenate([xf[r], xt[r]], axis=0)
            y = jnp.concatenate([y_in[p, c][0:feats], rep_in[p, c, 1]], axis=0)
            z = lax.dot_general(y, x, contract, preferred_element_type=F32)
            top = jnp.max(z, axis=0, keepdims=True)
            table = jnp.exp2(ALPHA * (z - top)).astype(BF16)
            tops.append(top)
            masses.append(jnp.dot(rep_in[p, c, 0], table, preferred_element_type=F32))
    best = fold_max(tops, masks)
    totals = [jnp.zeros((marginals, BLOCK), F32) for _ in range(blocks)]
    for top, mass, mask in zip(tops, masses, masks):
        scale = jnp.where(mask, jnp.exp2(ALPHA * (top - best)), 0.0)
        for n in range(blocks):
            totals[n] += scale[n : n + 1] * mass
    per = marginals // 8
    for n in range(blocks):
        s2_out[1 + per * n : 1 + per * (n + 1)] = totals[n].reshape(per, 8, BLOCK)
    s2_out[0] = best
    post(s2_out, s2_in, s_send.at[1], s_recv.at[1], device(blk, other))
    arrived(s2_in, s_send.at[1], s_recv.at[1])
    theirs = s2_in[0]
    peak = jnp.maximum(best, theirs)
    scale_own, scale_far = jnp.exp2(ALPHA * (best - peak)), jnp.exp2(ALPHA * (theirs - peak))
    used = peak > 0.5 * SENTINEL
    level = jnp.where(used, peak, 0.0)
    sums = []
    for n in range(blocks):
        lanes = slice(n * BLOCK, (n + 1) * BLOCK)
        far = s2_in[1 + per * n : 1 + per * (n + 1)].reshape(marginals, BLOCK)
        total = totals[n] * scale_own[n : n + 1] + far * scale_far[n : n + 1]
        total = jnp.where(used[n : n + 1], total, 1.0)
        weight = xw_ref[:, lanes].astype(F32) + 0.5
        bw[n] = (weight / total).astype(BF16)
        sums.append(total)
    shift_rows(level)
    col_sweep(1, bw)
    for n in range(blocks):
        lanes = slice(n * BLOCK, (n + 1) * BLOCK)
        weight = xw_ref[:, lanes].astype(F32) + 0.5
        real_out[:, lanes] = SMOOTH * (jnp.log(weight) - jnp.log(sums[n])) - level[n : n + 1]
    best, totals = col_fold(1)
    used = best > 0.5 * SENTINEL
    level = jnp.where(used, best, 0.0)
    for n in range(blocks):
        lanes = slice(n * BLOCK, (n + 1) * BLOCK)
        weight = yw_ref[:, lanes].astype(F32) + 0.5
        total = jnp.where(used[n : n + 1], totals[n], 1.0)
        synth_out[:, lanes] = SMOOTH * (jnp.log(weight) - jnp.log(total)) - level[n : n + 1]
    for copy in pending:
        copy.wait_send()


def shards(
    real_points, synth_points, real_cluster, synth_cluster, real_weight, synth_weight,
    pair_block, pair_row, pair_count,
):
    feats, count = real_points.shape
    blocks = count // BLOCK
    kept = real_weight.shape[0]
    marginals = -(-kept // TILE) * TILE
    if marginals > kept:
        grow = ((0, marginals - kept), (0, 0))
        real_weight, synth_weight = jnp.pad(real_weight, grow), jnp.pad(synth_weight, grow)
    peers, cap = pair_block.shape
    group = 2 * peers
    depth = feats + TILE
    vmem = pl.BlockSpec(memory_space=pltpu.VMEM)
    hbm = pl.BlockSpec(memory_space=pltpu.HBM)
    real_pot, synth_pot = pl.pallas_call(
        functools.partial(kernel, peers, cap, blocks, marginals, feats),
        out_shape=(
            jax.ShapeDtypeStruct((marginals, count), F32),
            jax.ShapeDtypeStruct((marginals, count), F32),
        ),
        in_specs=[hbm] * 9,
        out_specs=(vmem, vmem),
        scratch_shapes=[
            pltpu.VMEM((feats, count), BF16),
            pltpu.VMEM((feats, count), BF16),
            pltpu.VMEM((blocks, BLOCK), jnp.int32),
            pltpu.VMEM((blocks, BLOCK), jnp.int32),
            pltpu.VMEM((marginals, count), jnp.int32),
            pltpu.VMEM((marginals, count), jnp.int32),
            pltpu.SMEM((cap, peers), jnp.int32),
            pltpu.SMEM((cap, peers), jnp.int32),
            pltpu.SMEM((peers,), jnp.int32),
            pltpu.SemaphoreType.DMA((9,)),
            pltpu.VMEM((blocks, feats, BLOCK), BF16),
            pltpu.VMEM((blocks, TILE, BLOCK), BF16),
            pltpu.VMEM((blocks, TILE, BLOCK), BF16),
            pltpu.VMEM((blocks, marginals, BLOCK), BF16),
            pltpu.VMEM((blocks, depth, BLOCK), BF16),
            pltpu.VMEM((peers, cap, TILE, BLOCK), BF16),
            pltpu.VMEM((group, cap, TILE, BLOCK), BF16),
            pltpu.VMEM((peers, cap, depth, BLOCK), BF16),
            pltpu.VMEM((peers, cap, depth, BLOCK), BF16),
            pltpu.VMEM((2, blocks, BLOCK), F32),
            pltpu.VMEM((2, blocks, BLOCK), F32),
            pltpu.VMEM((2, peers, cap, marginals + 8, BLOCK), F32),
            pltpu.VMEM((2, group, cap, marginals + 8, BLOCK), F32),
            pltpu.VMEM((blocks, marginals, BLOCK), BF16),
            pltpu.VMEM((blocks, TILE, BLOCK), BF16),
            pltpu.VMEM((peers, cap, 2, TILE, BLOCK), BF16),
            pltpu.VMEM((peers, cap, 2, TILE, BLOCK), BF16),
            pltpu.VMEM((1 + marginals // 8 * blocks, 8, BLOCK), F32),
            pltpu.VMEM((1 + marginals // 8 * blocks, 8, BLOCK), F32),
            pltpu.VMEM((blocks, marginals, BLOCK), BF16),
            pltpu.SemaphoreType.DMA((3, group)),
            pltpu.SemaphoreType.DMA((3, group)),
            pltpu.SemaphoreType.DMA((2, peers)),
            pltpu.SemaphoreType.DMA((2, peers)),
            pltpu.SemaphoreType.DMA((2,)),
            pltpu.SemaphoreType.DMA((2,)),
        ],
        compiler_params=pltpu.CompilerParams(
            collective_id=0, has_side_effects=True, vmem_limit_bytes=62 * 1024 * 1024
        ),
    )(
        real_points, synth_points,
        real_cluster.reshape(blocks, BLOCK), synth_cluster.reshape(blocks, BLOCK),
        real_weight, synth_weight, pair_block.T, pair_row.T, pair_count,
    )
    return real_pot[:kept], synth_pot[:kept]


def solution(mesh):
    placed = (
        P(None, ("slab", "blk")),
        P(None, ("slab", "blk")),
        P(("slab", "blk")),
        P(("slab", "blk")),
        P("bag", ("slab", "blk")),
        P("bag", ("slab", "blk")),
        P(("slab", "blk", "sub"), None),
        P(("slab", "blk", "sub"), None),
        P(("slab", "blk", "sub")),
    )
    return jax.shard_map(
        shards,
        mesh=mesh,
        in_specs=placed,
        out_specs=(P("bag", ("slab", "blk")), P("bag", ("slab", "blk"))),
        check_vma=False,
    )
```

```python
import functools
import math

import jax
import jax.numpy as jnp
import ml_dtypes
from jax import lax
from jax.experimental import pallas as pl
from jax.experimental.pallas import tpu as pltpu
from jax.sharding import PartitionSpec as P

BLOCK = 128
SMOOTH = 0.1
PENALTY = 0.3
SENTINEL = -1e30
ALPHA = 1.0 / (SMOOTH * math.log(2.0))
HIGH = float(ml_dtypes.bfloat16(PENALTY))
LOW = float(ml_dtypes.bfloat16(PENALTY - HIGH))
TILE = 16
MESH = pl.DeviceIdType.MESH
F32 = jnp.float32
BF16 = jnp.bfloat16


def split3(value):
    first = value.astype(BF16).astype(F32)
    second = (value - first).astype(BF16).astype(F32)
    third = (value - first - second).astype(BF16).astype(F32)
    return first, second, third


def put_rows(tile, value, start):
    row = lax.broadcasted_iota(jnp.int32, tile.shape, 0)
    for offset, part in enumerate(split3(value)):
        tile = jnp.where(row == start + offset, part, tile)
    return tile


def fold_max(tops, masks):
    best = jnp.full((masks[0].shape[0], BLOCK), SENTINEL, F32)
    for top, mask in zip(tops, masks):
        best = jnp.maximum(best, jnp.where(mask, top, SENTINEL))
    return best


def kernel(
    peers, cap, blocks, marginals, feats,
    x_hbm, y_hbm, xc_hbm, yc_hbm, xw_hbm, yw_hbm, pb_hbm, pr_hbm, pc_hbm,
    real_out, synth_out,
    x_ref, y_ref, xc_ref, yc_ref, xw_ref, yw_ref, pb_ref, pr_ref, pc_ref, in_sem,
    xf, xt, xu, wr, ys, req_out, req_in, y_out, y_in,
    s1_out, s1_in, c_out, c_in, own_a, own_t, rep_out, rep_in, s2_out, s2_in, bw,
    big_send, big_recv, send, recv, s_send, s_recv,
):
    slab, blk, bag, sub = (lax.axis_index(name) for name in ("slab", "blk", "bag", "sub"))
    loads = [
        pltpu.make_async_copy(src, dst, in_sem.at[k])
        for k, (src, dst) in enumerate((
            (pb_hbm, pb_ref), (pc_hbm, pc_ref), (pr_hbm, pr_ref), (y_hbm, y_ref), (yc_hbm, yc_ref),
            (x_hbm, x_ref), (xc_hbm, xc_ref), (xw_hbm, xw_ref), (yw_hbm, yw_ref),
        ))
    ]
    for load in loads:
        load.start()
    other = 1 - sub
    mine = sub * peers + blk
    group = 2 * peers

    def device(p, s):
        return (slab, p, bag, s)

    others = [(lax.rem(blk + d, peers), s) for d in range(1, peers) for s in (sub, other)]
    others.append((blk, other))

    barrier = pltpu.get_barrier_semaphore()
    for p, s in others:
        pl.semaphore_signal(barrier, inc=1, device_id=device(p, s), device_id_type=MESH)

    for load in loads[:3]:
        load.wait()
    for p in range(peers):
        for c in range(cap):
            listed = c < pc_ref[p]
            wanted = jnp.where(listed, pb_ref[c, p], 99).astype(F32)
            req_out[p, c : c + 1] = jnp.full((1, BLOCK), wanted, F32)
    req_in[mine] = req_out[blk]
    pl.semaphore_wait(barrier, len(others))

    pending = []

    def post(src, dst, send_sem, recv_sem, target):
        copy = pltpu.make_async_remote_copy(
            src_ref=src, dst_ref=dst, send_sem=send_sem, recv_sem=recv_sem,
            device_id=target, device_id_type=MESH,
        )
        copy.start()
        pending.append(copy)

    def arrived(dst, send_sem, recv_sem):
        pltpu.make_async_remote_copy(
            src_ref=dst, dst_ref=dst, send_sem=send_sem, recv_sem=recv_sem,
            device_id=device(blk, other), device_id_type=MESH,
        ).wait_recv()

    for p, s in others:
        post(req_out.at[p], req_in.at[mine], big_send.at[0, s * peers + p], big_recv.at[0, mine],
             device(p, s))

    for load in loads[3:5]:
        load.wait()
    row = lax.broadcasted_iota(jnp.int32, (TILE, BLOCK), 0)
    cluster = jnp.where(row < 10, row - 6, row - 10)
    for n in range(blocks):
        lanes = slice(n * BLOCK, (n + 1) * BLOCK)
        y = y_ref[:, lanes]
        y32 = y.astype(F32)
        fy = -0.5 * jnp.sum(y32 * y32, axis=0, keepdims=True)
        hit = (row >= 6) & (row < 14) & (cluster == yc_ref[n : n + 1, :])
        tile = jnp.where(hit, jnp.where(row < 10, HIGH, LOW), 0.0)
        tile = jnp.where(row < 3, 1.0, tile)
        tile = put_rows(tile, fy, 3)
        ys[n, 0:feats] = y
        ys[n, feats:] = tile.astype(BF16)
    def asked_block(src, c):
        return jnp.broadcast_to(req_in[src, c : c + 1], (TILE, BLOCK)).astype(BF16)

    def answer(p):
        src = sub * peers + p
        for c in range(cap):
            asked = asked_block(src, c)
            value = ys[0].reshape(-1, TILE, BLOCK)
            for n in range(1, blocks):
                value = jnp.where((asked == n)[None], ys[n].reshape(-1, TILE, BLOCK), value)
            yield c, value.reshape(-1, BLOCK)

    for d in range(1, peers):
        p = lax.rem(blk + d, peers)
        src = sub * peers + p
        arrived(req_in.at[src], big_send.at[0, src], big_recv.at[0, src])
        for c, value in answer(p):
            y_out[p, c] = value
        post(y_out.at[p], y_in.at[blk], send.at[0, p], recv.at[0, blk], device(p, sub))
    for c, value in answer(blk):
        y_in[blk, c] = value

    for load in loads[5:]:
        load.wait()
    for n in range(blocks):
        lanes = slice(n * BLOCK, (n + 1) * BLOCK)
        x = x_ref[:, lanes]
        x32 = x.astype(F32)
        fx = -0.5 * jnp.sum(x32 * x32, axis=0, keepdims=True) - PENALTY
        hit = (row >= 6) & (row < 14) & (cluster == xc_ref[n : n + 1, :])
        tile = jnp.where(hit, 1.0, 0.0)
        tile = jnp.where((row >= 3) & (row < 6), 1.0, tile)
        tile = put_rows(tile, fx, 0)
        xf[n] = x
        xt[n] = tile.astype(BF16)
        wr[n] = (xw_ref[:, lanes].astype(F32) + 0.5).astype(BF16)

    order = [lax.rem(blk + d, peers) for d in range(peers)]
    far_first = order[1:] + order[:1]
    eight = lax.broadcasted_iota(jnp.int32, (blocks, BLOCK), 0)

    def row_of(p, c):
        return pr_ref[c, p]

    def row_mask(p, c):
        return eight == jnp.where(c < pc_ref[p], pr_ref[c, p], blocks)

    contract = (((0,), (0,)), ((), ()))
    slots = [(p, c) for p in order for c in range(cap)]
    masks = [row_mask(p, c) for p, c in slots]

    tops, sums = [], []
    for d, p in enumerate(order):
        if d == 1:
            for q in order[1:]:
                arrived(y_in.at[q], send.at[0, q], recv.at[0, q])
        for c in range(cap):
            r = row_of(p, c)
            x = jnp.concatenate([xf[r], xt[r]], axis=0)
            z = lax.dot_general(y_in[p, c], x, contract, preferred_element_type=F32)
            top = jnp.max(z, axis=0, keepdims=True)
            tops.append(top)
            sums.append(jnp.sum(jnp.exp2(ALPHA * (z - top)), axis=0, keepdims=True))
    best = fold_max(tops, masks)
    total = jnp.zeros((blocks, BLOCK), F32)
    for top, part, mask in zip(tops, sums, masks):
        total += jnp.where(mask, jnp.exp2(ALPHA * (top - best)) * part, 0.0)
    s1_out[0] = best
    s1_out[1] = total
    post(s1_out, s1_in, s_send.at[0], s_recv.at[0], device(blk, other))
    arrived(s1_in, s_send.at[0], s_recv.at[0])
    peak = jnp.maximum(best, s1_in[0])
    total = total * jnp.exp2(ALPHA * (best - peak)) + s1_in[1] * jnp.exp2(ALPHA * (s1_in[0] - peak))
    used = peak > 0.5 * SENTINEL
    level = jnp.where(used, peak + jnp.log(jnp.where(used, total, 1.0)) * SMOOTH, 0.0)

    def shift_rows(level):
        for n in range(blocks):
            lanes = slice(n * BLOCK, (n + 1) * BLOCK)
            tile = xt[n].astype(F32)
            base = tile[0:1] + tile[1:2] + tile[2:3]
            xu[n] = put_rows(tile, base - level[n : n + 1], 0).astype(BF16)

    def col_sweep(turn, factor):
        def masses(p):
            for c in range(cap):
                r = row_of(p, c)
                x = jnp.concatenate([xf[r], xu[r]], axis=0)
                z = lax.dot_general(x, y_in[p, c], contract, preferred_element_type=F32)
                top = jnp.max(z, axis=0, keepdims=True)
                table = jnp.exp2(ALPHA * (z - top)).astype(BF16)
                mass = jnp.dot(factor[r], table, preferred_element_type=F32)
                yield c, mass.astype(BF16), top

        def deliver(p, s):
            post(c_out.at[turn, p], c_in.at[turn, mine], big_send.at[1 + turn, s * peers + p],
                 big_recv.at[1 + turn, mine], device(p, s))

        def keep(p, targets):
            tile = jnp.zeros((TILE, BLOCK), F32)
            for c, mass, top in masses(p):
                tile = put_rows(tile, top, 3 * c)
                for target in targets:
                    target[c * marginals : (c + 1) * marginals] = mass
            for target in targets:
                target[cap * marginals :] = tile.astype(BF16)

        for p in order[1:]:
            keep(p, [c_out.at[turn, p]])
        for p in order[1:]:
            deliver(p, sub)
            deliver(p, other)
        keep(blk, [c_out.at[turn, blk], c_in.at[turn, mine]])
        deliver(blk, other)

    def col_fold(turn):
        sources = [mine, other * peers + blk]
        sources += [s * peers + p for p in order[1:] for s in (sub, other)]
        tops, hits = [], []
        for d, src in enumerate(sources):
            if d:
                arrived(c_in.at[turn, src], big_send.at[1 + turn, src], big_recv.at[1 + turn, src])
                if turn == 0 and d % 2 == 1:
                    arrived(req_in.at[src], big_send.at[0, src], big_recv.at[0, src])
            tile = c_in[turn, src, cap * marginals :].astype(F32)
            for c in range(cap):
                tops.append(tile[3 * c : 3 * c + 1] + tile[3 * c + 1 : 3 * c + 2] + tile[3 * c + 2 : 3 * c + 3])
                hits.append(req_in[src, c : c + 1] == eight.astype(F32))
        best = fold_max(tops, hits)
        totals = [jnp.zeros((marginals, BLOCK), F32) for _ in range(blocks)]
        k = 0
        for src in sources:
            for c in range(cap):
                scale = jnp.where(hits[k], jnp.exp2(ALPHA * (tops[k] - best)), 0.0)
                mass = c_in[turn, src, c * marginals : (c + 1) * marginals].astype(F32)
                for n in range(blocks):
                    totals[n] += scale[n : n + 1] * mass
                k += 1
        return best, totals

    shift_rows(level)
    col_sweep(0, wr)
    best, totals = col_fold(0)
    used = best > 0.5 * SENTINEL
    level = jnp.where(used, best, 0.0)
    for n in range(blocks):
        lanes = slice(n * BLOCK, (n + 1) * BLOCK)
        some = used[n : n + 1]
        weight = yw_ref[:, lanes].astype(F32) + 0.5
        own_a[n] = (weight / jnp.where(some, totals[n], 1.0)).astype(BF16)
        tile = ys[n, feats:].astype(F32)
        base = tile[3:4] + tile[4:5] + tile[5:6]
        own_t[n] = put_rows(tile, base - level[n : n + 1], 3).astype(BF16)
    for d, p in enumerate(far_first):
        src = sub * peers + p
        for c in range(cap):
            asked = asked_block(src, c)
            factor, tile = own_a[0], own_t[0]
            for n in range(1, blocks):
                hit = asked == n
                factor = jnp.where(hit, own_a[n], factor)
                tile = jnp.where(hit, own_t[n], tile)
            target = rep_in if d == peers - 1 else rep_out
            target[p, c, 0] = factor
            target[p, c, 1] = tile
        if d < peers - 1:
            post(rep_out.at[p], rep_in.at[blk], send.at[1, p], recv.at[1, blk], device(p, sub))

    tops, masses = [], []
    for d, p in enumerate(order):
        if d == 1:
            for q in order[1:]:
                arrived(rep_in.at[q], send.at[1, q], recv.at[1, q])
        for c in range(cap):
            r = row_of(p, c)
            x = jnp.concatenate([xf[r], xt[r]], axis=0)
            y = jnp.concatenate([y_in[p, c][0:feats], rep_in[p, c, 1]], axis=0)
            z = lax.dot_general(y, x, contract, preferred_element_type=F32)
            top = jnp.max(z, axis=0, keepdims=True)
            table = jnp.exp2(ALPHA * (z - top)).astype(BF16)
            tops.append(top)
            masses.append(jnp.dot(rep_in[p, c, 0], table, preferred_element_type=F32))
    best = fold_max(tops, masks)
    totals = [jnp.zeros((marginals, BLOCK), F32) for _ in range(blocks)]
    for top, mass, mask in zip(tops, masses, masks):
        scale = jnp.where(mask, jnp.exp2(ALPHA * (top - best)), 0.0)
        for n in range(blocks):
            totals[n] += scale[n : n + 1] * mass
    per = marginals // 8
    for n in range(blocks):
        s2_out[1 + per * n : 1 + per * (n + 1)] = totals[n].reshape(per, 8, BLOCK)
    s2_out[0] = best
    post(s2_out, s2_in, s_send.at[1], s_recv.at[1], device(blk, other))
    arrived(s2_in, s_send.at[1], s_recv.at[1])
    theirs = s2_in[0]
    peak = jnp.maximum(best, theirs)
    scale_own, scale_far = jnp.exp2(ALPHA * (best - peak)), jnp.exp2(ALPHA * (theirs - peak))
    used = peak > 0.5 * SENTINEL
    level = jnp.where(used, peak, 0.0)
    sums = []
    for n in range(blocks):
        lanes = slice(n * BLOCK, (n + 1) * BLOCK)
        far = s2_in[1 + per * n : 1 + per * (n + 1)].reshape(marginals, BLOCK)
        total = totals[n] * scale_own[n : n + 1] + far * scale_far[n : n + 1]
        total = jnp.where(used[n : n + 1], total, 1.0)
        weight = xw_ref[:, lanes].astype(F32) + 0.5
        bw[n] = (weight / total).astype(BF16)
        sums.append(total)
    shift_rows(level)
    col_sweep(1, bw)
    for n in range(blocks):
        lanes = slice(n * BLOCK, (n + 1) * BLOCK)
        weight = xw_ref[:, lanes].astype(F32) + 0.5
        real_out[:, lanes] = SMOOTH * (jnp.log(weight) - jnp.log(sums[n])) - level[n : n + 1]
    best, totals = col_fold(1)
    used = best > 0.5 * SENTINEL
    level = jnp.where(used, best, 0.0)
    for n in range(blocks):
        lanes = slice(n * BLOCK, (n + 1) * BLOCK)
        weight = yw_ref[:, lanes].astype(F32) + 0.5
        total = jnp.where(used[n : n + 1], totals[n], 1.0)
        synth_out[:, lanes] = SMOOTH * (jnp.log(weight) - jnp.log(total)) - level[n : n + 1]
    for copy in pending:
        copy.wait_send()


def shards(
    real_points, synth_points, real_cluster, synth_cluster, real_weight, synth_weight,
    pair_block, pair_row, pair_count,
):
    feats, count = real_points.shape
    blocks = count // BLOCK
    kept = real_weight.shape[0]
    marginals = -(-kept // TILE) * TILE
    if marginals > kept:
        grow = ((0, marginals - kept), (0, 0))
        real_weight, synth_weight = jnp.pad(real_weight, grow), jnp.pad(synth_weight, grow)
    peers, cap = pair_block.shape
    group = 2 * peers
    depth = feats + TILE
    vmem = pl.BlockSpec(memory_space=pltpu.VMEM)
    hbm = pl.BlockSpec(memory_space=pltpu.HBM)
    real_pot, synth_pot = pl.pallas_call(
        functools.partial(kernel, peers, cap, blocks, marginals, feats),
        out_shape=(
            jax.ShapeDtypeStruct((marginals, count), F32),
            jax.ShapeDtypeStruct((marginals, count), F32),
        ),
        in_specs=[hbm] * 9,
        out_specs=(vmem, vmem),
        scratch_shapes=[
            pltpu.VMEM((feats, count), BF16),
            pltpu.VMEM((feats, count), BF16),
            pltpu.VMEM((blocks, BLOCK), jnp.int32),
            pltpu.VMEM((blocks, BLOCK), jnp.int32),
            pltpu.VMEM((marginals, count), jnp.int32),
            pltpu.VMEM((marginals, count), jnp.int32),
            pltpu.SMEM((cap, peers), jnp.int32),
            pltpu.SMEM((cap, peers), jnp.int32),
            pltpu.SMEM((peers,), jnp.int32),
            pltpu.SemaphoreType.DMA((9,)),
            pltpu.VMEM((blocks, feats, BLOCK), BF16),
            pltpu.VMEM((blocks, TILE, BLOCK), BF16),
            pltpu.VMEM((blocks, TILE, BLOCK), BF16),
            pltpu.VMEM((blocks, marginals, BLOCK), BF16),
            pltpu.VMEM((blocks, depth, BLOCK), BF16),
            pltpu.VMEM((peers, cap, BLOCK), F32),
            pltpu.VMEM((group, cap, BLOCK), F32),
            pltpu.VMEM((peers, cap, depth, BLOCK), BF16),
            pltpu.VMEM((peers, cap, depth, BLOCK), BF16),
            pltpu.VMEM((2, blocks, BLOCK), F32),
            pltpu.VMEM((2, blocks, BLOCK), F32),
            pltpu.VMEM((2, peers, cap * marginals + TILE, BLOCK), BF16),
            pltpu.VMEM((2, group, cap * marginals + TILE, BLOCK), BF16),
            pltpu.VMEM((blocks, marginals, BLOCK), BF16),
            pltpu.VMEM((blocks, TILE, BLOCK), BF16),
            pltpu.VMEM((peers, cap, 2, TILE, BLOCK), BF16),
            pltpu.VMEM((peers, cap, 2, TILE, BLOCK), BF16),
            pltpu.VMEM((1 + marginals // 8 * blocks, 8, BLOCK), F32),
            pltpu.VMEM((1 + marginals // 8 * blocks, 8, BLOCK), F32),
            pltpu.VMEM((blocks, marginals, BLOCK), BF16),
            pltpu.SemaphoreType.DMA((3, group)),
            pltpu.SemaphoreType.DMA((3, group)),
            pltpu.SemaphoreType.DMA((2, peers)),
            pltpu.SemaphoreType.DMA((2, peers)),
            pltpu.SemaphoreType.DMA((2,)),
            pltpu.SemaphoreType.DMA((2,)),
        ],
        compiler_params=pltpu.CompilerParams(
            collective_id=0, has_side_effects=True, vmem_limit_bytes=62 * 1024 * 1024
        ),
    )(
        real_points, synth_points,
        real_cluster.reshape(blocks, BLOCK), synth_cluster.reshape(blocks, BLOCK),
        real_weight, synth_weight, pair_block.T, pair_row.T, pair_count,
    )
    return real_pot[:kept], synth_pot[:kept]


def solution(mesh):
    placed = (
        P(None, ("slab", "blk")),
        P(None, ("slab", "blk")),
        P(("slab", "blk")),
        P(("slab", "blk")),
        P("bag", ("slab", "blk")),
        P("bag", ("slab", "blk")),
        P(("slab", "blk", "sub"), None),
        P(("slab", "blk", "sub"), None),
        P(("slab", "blk", "sub")),
    )
    return jax.shard_map(
        shards,
        mesh=mesh,
        in_specs=placed,
        out_specs=(P("bag", ("slab", "blk")), P("bag", ("slab", "blk"))),
        check_vma=False,
    )
```

```python
import functools
import math

import jax
import jax.numpy as jnp
import ml_dtypes
from jax import lax
from jax.experimental import pallas as pl
from jax.experimental.pallas import tpu as pltpu
from jax.sharding import PartitionSpec as P

BLOCK = 128
SMOOTH = 0.1
PENALTY = 0.3
SENTINEL = -1e30
ALPHA = 1.0 / (SMOOTH * math.log(2.0))
HIGH = float(ml_dtypes.bfloat16(PENALTY))
LOW = float(ml_dtypes.bfloat16(PENALTY - HIGH))
TILE = 16
MESH = pl.DeviceIdType.MESH
F32 = jnp.float32
BF16 = jnp.bfloat16


def split3(value):
    first = value.astype(BF16).astype(F32)
    second = (value - first).astype(BF16).astype(F32)
    third = (value - first - second).astype(BF16).astype(F32)
    return first, second, third


def put_rows(tile, value, start):
    row = lax.broadcasted_iota(jnp.int32, tile.shape, 0)
    for offset, part in enumerate(split3(value)):
        tile = jnp.where(row == start + offset, part, tile)
    return tile


def fold_max(tops, masks):
    best = jnp.full((masks[0].shape[0], BLOCK), SENTINEL, F32)
    for top, mask in zip(tops, masks):
        best = jnp.maximum(best, jnp.where(mask, top, SENTINEL))
    return best


def kernel(
    peers, cap, blocks, marginals, feats,
    x_hbm, y_hbm, xc_hbm, yc_hbm, xw_hbm, yw_hbm, pb_hbm, pr_hbm, pc_hbm,
    real_hbm, synth_hbm,
    x_ref, y_ref, xc_ref, yc_ref, xw_ref, yw_ref, pb_ref, pr_ref, pc_ref, in_sem,
    real_out, synth_out, out_sem,
    xf, xt, xu, wr, ys, req_out, req_in, y_out, y_in,
    s1_out, s1_in, c_out, c_in, own_a, own_t, rep_out, rep_in, s2_out, s2_in, bw,
    big_send, big_recv, send, recv, s_send, s_recv,
):
    slab, blk, bag, sub = (lax.axis_index(name) for name in ("slab", "blk", "bag", "sub"))
    loads = [
        pltpu.make_async_copy(src, dst, in_sem.at[k])
        for k, (src, dst) in enumerate((
            (pb_hbm, pb_ref), (pc_hbm, pc_ref), (pr_hbm, pr_ref), (y_hbm, y_ref), (yc_hbm, yc_ref),
            (x_hbm, x_ref), (xc_hbm, xc_ref), (xw_hbm, xw_ref), (yw_hbm, yw_ref),
        ))
    ]
    for load in loads:
        load.start()
    other = 1 - sub
    mine = sub * peers + blk
    group = 2 * peers

    def device(p, s):
        return (slab, p, bag, s)

    others = [(lax.rem(blk + d, peers), s) for d in range(1, peers) for s in (sub, other)]
    others.append((blk, other))

    barrier = pltpu.get_barrier_semaphore()
    for p, s in others:
        pl.semaphore_signal(barrier, inc=1, device_id=device(p, s), device_id_type=MESH)

    for load in loads[:3]:
        load.wait()
    for p in range(peers):
        for c in range(cap):
            listed = c < pc_ref[p]
            wanted = jnp.where(listed, pb_ref[c, p], 99).astype(F32)
            req_out[p, c : c + 1] = jnp.full((1, BLOCK), wanted, F32)
    req_in[mine] = req_out[blk]
    pl.semaphore_wait(barrier, len(others))

    pending = []

    def post(src, dst, send_sem, recv_sem, target):
        copy = pltpu.make_async_remote_copy(
            src_ref=src, dst_ref=dst, send_sem=send_sem, recv_sem=recv_sem,
            device_id=target, device_id_type=MESH,
        )
        copy.start()
        pending.append(copy)

    def arrived(dst, send_sem, recv_sem):
        pltpu.make_async_remote_copy(
            src_ref=dst, dst_ref=dst, send_sem=send_sem, recv_sem=recv_sem,
            device_id=device(blk, other), device_id_type=MESH,
        ).wait_recv()

    for p, s in others:
        post(req_out.at[p], req_in.at[mine], big_send.at[0, s * peers + p], big_recv.at[0, mine],
             device(p, s))

    for load in loads[3:5]:
        load.wait()
    row = lax.broadcasted_iota(jnp.int32, (TILE, BLOCK), 0)
    cluster = jnp.where(row < 10, row - 6, row - 10)
    for n in range(blocks):
        lanes = slice(n * BLOCK, (n + 1) * BLOCK)
        y = y_ref[:, lanes]
        y32 = y.astype(F32)
        fy = -0.5 * jnp.sum(y32 * y32, axis=0, keepdims=True)
        hit = (row >= 6) & (row < 14) & (cluster == yc_ref[n : n + 1, :])
        tile = jnp.where(hit, jnp.where(row < 10, HIGH, LOW), 0.0)
        tile = jnp.where(row < 3, 1.0, tile)
        tile = put_rows(tile, fy, 3)
        ys[n, 0:feats] = y
        ys[n, feats:] = tile.astype(BF16)
    def asked_block(src, c):
        return jnp.broadcast_to(req_in[src, c : c + 1], (TILE, BLOCK)).astype(BF16)

    def answer(p):
        src = sub * peers + p
        for c in range(cap):
            asked = asked_block(src, c)
            value = ys[0].reshape(-1, TILE, BLOCK)
            for n in range(1, blocks):
                value = jnp.where((asked == n)[None], ys[n].reshape(-1, TILE, BLOCK), value)
            yield c, value.reshape(-1, BLOCK)

    for d in range(1, peers):
        p = lax.rem(blk + d, peers)
        src = sub * peers + p
        arrived(req_in.at[src], big_send.at[0, src], big_recv.at[0, src])
        for c, value in answer(p):
            y_out[p, c] = value
        post(y_out.at[p], y_in.at[blk], send.at[0, p], recv.at[0, blk], device(p, sub))
    for c, value in answer(blk):
        y_in[blk, c] = value

    for load in loads[5:]:
        load.wait()
    for n in range(blocks):
        lanes = slice(n * BLOCK, (n + 1) * BLOCK)
        x = x_ref[:, lanes]
        x32 = x.astype(F32)
        fx = -0.5 * jnp.sum(x32 * x32, axis=0, keepdims=True) - PENALTY
        hit = (row >= 6) & (row < 14) & (cluster == xc_ref[n : n + 1, :])
        tile = jnp.where(hit, 1.0, 0.0)
        tile = jnp.where((row >= 3) & (row < 6), 1.0, tile)
        tile = put_rows(tile, fx, 0)
        xf[n] = x
        xt[n] = tile.astype(BF16)
        wr[n] = (xw_ref[:, lanes].astype(F32) + 0.5).astype(BF16)

    order = [lax.rem(blk + d, peers) for d in range(peers)]
    far_first = order[1:] + order[:1]
    eight = lax.broadcasted_iota(jnp.int32, (blocks, BLOCK), 0)

    def row_of(p, c):
        return pr_ref[c, p]

    def row_mask(p, c):
        return eight == jnp.where(c < pc_ref[p], pr_ref[c, p], blocks)

    contract = (((0,), (0,)), ((), ()))
    slots = [(p, c) for p in order for c in range(cap)]
    masks = [row_mask(p, c) for p, c in slots]

    tops, sums = [], []
    for d, p in enumerate(order):
        if d == 1:
            for q in order[1:]:
                arrived(y_in.at[q], send.at[0, q], recv.at[0, q])
        for c in range(cap):
            r = row_of(p, c)
            x = jnp.concatenate([xf[r], xt[r]], axis=0)
            z = lax.dot_general(y_in[p, c], x, contract, preferred_element_type=F32)
            top = jnp.max(z, axis=0, keepdims=True)
            tops.append(top)
            sums.append(jnp.sum(jnp.exp2(ALPHA * (z - top)), axis=0, keepdims=True))
    best = fold_max(tops, masks)
    total = jnp.zeros((blocks, BLOCK), F32)
    for top, part, mask in zip(tops, sums, masks):
        total += jnp.where(mask, jnp.exp2(ALPHA * (top - best)) * part, 0.0)
    s1_out[0] = best
    s1_out[1] = total
    post(s1_out, s1_in, s_send.at[0], s_recv.at[0], device(blk, other))
    arrived(s1_in, s_send.at[0], s_recv.at[0])
    peak = jnp.maximum(best, s1_in[0])
    total = total * jnp.exp2(ALPHA * (best - peak)) + s1_in[1] * jnp.exp2(ALPHA * (s1_in[0] - peak))
    used = peak > 0.5 * SENTINEL
    level = jnp.where(used, peak + jnp.log(jnp.where(used, total, 1.0)) * SMOOTH, 0.0)

    def shift_rows(level):
        for n in range(blocks):
            lanes = slice(n * BLOCK, (n + 1) * BLOCK)
            tile = xt[n].astype(F32)
            base = tile[0:1] + tile[1:2] + tile[2:3]
            xu[n] = put_rows(tile, base - level[n : n + 1], 0).astype(BF16)

    def col_sweep(turn, factor):
        def masses(p):
            for c in range(cap):
                r = row_of(p, c)
                x = jnp.concatenate([xf[r], xu[r]], axis=0)
                z = lax.dot_general(x, y_in[p, c], contract, preferred_element_type=F32)
                top = jnp.max(z, axis=0, keepdims=True)
                table = jnp.exp2(ALPHA * (z - top)).astype(BF16)
                mass = jnp.dot(factor[r], table, preferred_element_type=F32)
                yield c, mass.astype(BF16), top

        def deliver(p, s):
            post(c_out.at[turn, p], c_in.at[turn, mine], big_send.at[1 + turn, s * peers + p],
                 big_recv.at[1 + turn, mine], device(p, s))

        def keep(p, targets):
            tile = jnp.zeros((TILE, BLOCK), F32)
            for c, mass, top in masses(p):
                tile = put_rows(tile, top, 3 * c)
                for target in targets:
                    target[c * marginals : (c + 1) * marginals] = mass
            for target in targets:
                target[cap * marginals :] = tile.astype(BF16)

        for p in order[1:]:
            keep(p, [c_out.at[turn, p]])
        for p in order[1:]:
            deliver(p, sub)
            deliver(p, other)
        keep(blk, [c_out.at[turn, blk], c_in.at[turn, mine]])
        deliver(blk, other)

    def col_fold(turn):
        sources = [mine, other * peers + blk]
        sources += [s * peers + p for p in order[1:] for s in (sub, other)]
        tops, hits = [], []
        for d, src in enumerate(sources):
            if d:
                arrived(c_in.at[turn, src], big_send.at[1 + turn, src], big_recv.at[1 + turn, src])
                if turn == 0 and d % 2 == 1:
                    arrived(req_in.at[src], big_send.at[0, src], big_recv.at[0, src])
            tile = c_in[turn, src, cap * marginals :].astype(F32)
            for c in range(cap):
                tops.append(tile[3 * c : 3 * c + 1] + tile[3 * c + 1 : 3 * c + 2] + tile[3 * c + 2 : 3 * c + 3])
                hits.append(req_in[src, c : c + 1] == eight.astype(F32))
        best = fold_max(tops, hits)
        totals = [jnp.zeros((marginals, BLOCK), F32) for _ in range(blocks)]
        k = 0
        for src in sources:
            for c in range(cap):
                scale = jnp.where(hits[k], jnp.exp2(ALPHA * (tops[k] - best)), 0.0)
                mass = c_in[turn, src, c * marginals : (c + 1) * marginals].astype(F32)
                for n in range(blocks):
                    totals[n] += scale[n : n + 1] * mass
                k += 1
        return best, totals

    shift_rows(level)
    col_sweep(0, wr)
    best, totals = col_fold(0)
    used = best > 0.5 * SENTINEL
    level = jnp.where(used, best, 0.0)
    for n in range(blocks):
        lanes = slice(n * BLOCK, (n + 1) * BLOCK)
        some = used[n : n + 1]
        weight = yw_ref[:, lanes].astype(F32) + 0.5
        own_a[n] = (weight / jnp.where(some, totals[n], 1.0)).astype(BF16)
        tile = ys[n, feats:].astype(F32)
        base = tile[3:4] + tile[4:5] + tile[5:6]
        own_t[n] = put_rows(tile, base - level[n : n + 1], 3).astype(BF16)
    for d, p in enumerate(far_first):
        src = sub * peers + p
        for c in range(cap):
            asked = asked_block(src, c)
            factor, tile = own_a[0], own_t[0]
            for n in range(1, blocks):
                hit = asked == n
                factor = jnp.where(hit, own_a[n], factor)
                tile = jnp.where(hit, own_t[n], tile)
            target = rep_in if d == peers - 1 else rep_out
            target[p, c, 0] = factor
            target[p, c, 1] = tile
        if d < peers - 1:
            post(rep_out.at[p], rep_in.at[blk], send.at[1, p], recv.at[1, blk], device(p, sub))

    tops, masses = [], []
    for d, p in enumerate(order):
        if d == 1:
            for q in order[1:]:
                arrived(rep_in.at[q], send.at[1, q], recv.at[1, q])
        for c in range(cap):
            r = row_of(p, c)
            x = jnp.concatenate([xf[r], xt[r]], axis=0)
            y = jnp.concatenate([y_in[p, c][0:feats], rep_in[p, c, 1]], axis=0)
            z = lax.dot_general(y, x, contract, preferred_element_type=F32)
            top = jnp.max(z, axis=0, keepdims=True)
            table = jnp.exp2(ALPHA * (z - top)).astype(BF16)
            tops.append(top)
            masses.append(jnp.dot(rep_in[p, c, 0], table, preferred_element_type=F32))
    best = fold_max(tops, masks)
    totals = [jnp.zeros((marginals, BLOCK), F32) for _ in range(blocks)]
    for top, mass, mask in zip(tops, masses, masks):
        scale = jnp.where(mask, jnp.exp2(ALPHA * (top - best)), 0.0)
        for n in range(blocks):
            totals[n] += scale[n : n + 1] * mass
    per = marginals // 8
    for n in range(blocks):
        s2_out[1 + per * n : 1 + per * (n + 1)] = totals[n].reshape(per, 8, BLOCK)
    s2_out[0] = best
    post(s2_out, s2_in, s_send.at[1], s_recv.at[1], device(blk, other))
    arrived(s2_in, s_send.at[1], s_recv.at[1])
    theirs = s2_in[0]
    peak = jnp.maximum(best, theirs)
    scale_own, scale_far = jnp.exp2(ALPHA * (best - peak)), jnp.exp2(ALPHA * (theirs - peak))
    used = peak > 0.5 * SENTINEL
    level = jnp.where(used, peak, 0.0)
    sums = []
    for n in range(blocks):
        lanes = slice(n * BLOCK, (n + 1) * BLOCK)
        far = s2_in[1 + per * n : 1 + per * (n + 1)].reshape(marginals, BLOCK)
        total = totals[n] * scale_own[n : n + 1] + far * scale_far[n : n + 1]
        total = jnp.where(used[n : n + 1], total, 1.0)
        weight = xw_ref[:, lanes].astype(F32) + 0.5
        bw[n] = (weight / total).astype(BF16)
        sums.append(total)
    shift_rows(level)
    col_sweep(1, bw)
    for n in range(blocks):
        lanes = slice(n * BLOCK, (n + 1) * BLOCK)
        weight = xw_ref[:, lanes].astype(F32) + 0.5
        real_out[:, lanes] = SMOOTH * (jnp.log(weight) - jnp.log(sums[n])) - level[n : n + 1]
    store_real = pltpu.make_async_copy(real_out, real_hbm, out_sem.at[0])
    store_real.start()
    best, totals = col_fold(1)
    used = best > 0.5 * SENTINEL
    level = jnp.where(used, best, 0.0)
    for n in range(blocks):
        lanes = slice(n * BLOCK, (n + 1) * BLOCK)
        weight = yw_ref[:, lanes].astype(F32) + 0.5
        total = jnp.where(used[n : n + 1], totals[n], 1.0)
        synth_out[:, lanes] = SMOOTH * (jnp.log(weight) - jnp.log(total)) - level[n : n + 1]
    store_synth = pltpu.make_async_copy(synth_out, synth_hbm, out_sem.at[1])
    store_synth.start()
    for copy in pending:
        copy.wait_send()
    store_real.wait()
    store_synth.wait()


def shards(
    real_points, synth_points, real_cluster, synth_cluster, real_weight, synth_weight,
    pair_block, pair_row, pair_count,
):
    feats, count = real_points.shape
    blocks = count // BLOCK
    kept = real_weight.shape[0]
    marginals = -(-kept // TILE) * TILE
    if marginals > kept:
        grow = ((0, marginals - kept), (0, 0))
        real_weight, synth_weight = jnp.pad(real_weight, grow), jnp.pad(synth_weight, grow)
    peers, cap = pair_block.shape
    group = 2 * peers
    depth = feats + TILE
    hbm = pl.BlockSpec(memory_space=pltpu.HBM)
    real_pot, synth_pot = pl.pallas_call(
        functools.partial(kernel, peers, cap, blocks, marginals, feats),
        out_shape=(
            jax.ShapeDtypeStruct((marginals, count), F32),
            jax.ShapeDtypeStruct((marginals, count), F32),
        ),
        in_specs=[hbm] * 9,
        out_specs=(hbm, hbm),
        scratch_shapes=[
            pltpu.VMEM((feats, count), BF16),
            pltpu.VMEM((feats, count), BF16),
            pltpu.VMEM((blocks, BLOCK), jnp.int32),
            pltpu.VMEM((blocks, BLOCK), jnp.int32),
            pltpu.VMEM((marginals, count), jnp.int32),
            pltpu.VMEM((marginals, count), jnp.int32),
            pltpu.SMEM((cap, peers), jnp.int32),
            pltpu.SMEM((cap, peers), jnp.int32),
            pltpu.SMEM((peers,), jnp.int32),
            pltpu.SemaphoreType.DMA((9,)),
            pltpu.VMEM((marginals, count), F32),
            pltpu.VMEM((marginals, count), F32),
            pltpu.SemaphoreType.DMA((2,)),
            pltpu.VMEM((blocks, feats, BLOCK), BF16),
            pltpu.VMEM((blocks, TILE, BLOCK), BF16),
            pltpu.VMEM((blocks, TILE, BLOCK), BF16),
            pltpu.VMEM((blocks, marginals, BLOCK), BF16),
            pltpu.VMEM((blocks, depth, BLOCK), BF16),
            pltpu.VMEM((peers, cap, BLOCK), F32),
            pltpu.VMEM((group, cap, BLOCK), F32),
            pltpu.VMEM((peers, cap, depth, BLOCK), BF16),
            pltpu.VMEM((peers, cap, depth, BLOCK), BF16),
            pltpu.VMEM((2, blocks, BLOCK), F32),
            pltpu.VMEM((2, blocks, BLOCK), F32),
            pltpu.VMEM((2, peers, cap * marginals + TILE, BLOCK), BF16),
            pltpu.VMEM((2, group, cap * marginals + TILE, BLOCK), BF16),
            pltpu.VMEM((blocks, marginals, BLOCK), BF16),
            pltpu.VMEM((blocks, TILE, BLOCK), BF16),
            pltpu.VMEM((peers, cap, 2, TILE, BLOCK), BF16),
            pltpu.VMEM((peers, cap, 2, TILE, BLOCK), BF16),
            pltpu.VMEM((1 + marginals // 8 * blocks, 8, BLOCK), F32),
            pltpu.VMEM((1 + marginals // 8 * blocks, 8, BLOCK), F32),
            pltpu.VMEM((blocks, marginals, BLOCK), BF16),
            pltpu.SemaphoreType.DMA((3, group)),
            pltpu.SemaphoreType.DMA((3, group)),
            pltpu.SemaphoreType.DMA((2, peers)),
            pltpu.SemaphoreType.DMA((2, peers)),
            pltpu.SemaphoreType.DMA((2,)),
            pltpu.SemaphoreType.DMA((2,)),
        ],
        compiler_params=pltpu.CompilerParams(
            collective_id=0, has_side_effects=True, vmem_limit_bytes=62 * 1024 * 1024
        ),
    )(
        real_points, synth_points,
        real_cluster.reshape(blocks, BLOCK), synth_cluster.reshape(blocks, BLOCK),
        real_weight, synth_weight, pair_block.T, pair_row.T, pair_count,
    )
    return real_pot[:kept], synth_pot[:kept]


def solution(mesh):
    placed = (
        P(None, ("slab", "blk")),
        P(None, ("slab", "blk")),
        P(("slab", "blk")),
        P(("slab", "blk")),
        P("bag", ("slab", "blk")),
        P("bag", ("slab", "blk")),
        P(("slab", "blk", "sub"), None),
        P(("slab", "blk", "sub"), None),
        P(("slab", "blk", "sub")),
    )
    return jax.shard_map(
        shards,
        mesh=mesh,
        in_specs=placed,
        out_specs=(P("bag", ("slab", "blk")), P("bag", ("slab", "blk"))),
        check_vma=False,
    )
```
